512 devices in a mesh: col: 16 (over z), row: 32 (over x, y, core).
Axes of the slice: x: 4, y: 4, z: 16, core: 2. Of those that a mesh axis runs over, the one named last changes fastest.
Arguments:
- out_grad: bfloat16 [131072, 256], P(('col', 'row')), may hold values from -6 to 6
- relu_mask: int32 [131072, 256], P(('col', 'row')), may hold values 0 or 1
- features: bfloat16 [131072, 256], P(('col', 'row')), may hold values from -0.0390625 to 0.0390625
- weight: bfloat16 [256, 256], replicated, may hold values from -0.375 to 0.375
- tile_values: bfloat16 [16, 32, 96, 128, 128], P('col', 'row'), may hold values from -0.125 to 0.125
- tile_index: int32 [16, 32, 96], P('col', 'row'), may hold values from 0 to 2047, as said below
- tile_count: int32 [16, 32], P('col', 'row'), may hold values from 1 to 96, as said below
Outputs:
- input_grad: bfloat16 [131072, 256], P(('col', 'row'))
- weight_grad: float32 [256, 256], replicated
The draws below stay inside these ranges and needn't reach their ends.
Inputs may be any that keep to these rules, and one draw needn't show every extreme that they name: `tile_index`: within one device the 96 entries are distinct positions of its grid of 64 x 32 tiles. `tile_count`: at least 1; some device in every draw has all 96 slots live.
All inputs are finite; a program needn't handle non-finite values. No bound on the sum of `relu_mask` on one device may be relied on, other than what follows from the above.
Results may differ from the reference program's by a relative error of at most 0.0049.
Values may be sent and summed in bfloat16 or wider, within the bound.
A program may use at most 128 MiB of HBM per device.

```python
import jax
import jax.numpy as jnp
from jax import lax

F = 256
BLK = 128
SEGB = 2
SLOTS = 96
STRIPE = 64
COLB = 32
NODES = 131072
N_COL = 16
N_ROW = 32


def draw_tile_index(key, part):
    key = jax.random.fold_in(key, 11)
    device_keys = jax.random.split(key, N_COL * N_ROW)
    grid_size = STRIPE * COLB

    def one_device(device_key):
        return jax.random.permutation(device_key, grid_size)[:SLOTS]
    chosen = jax.vmap(one_device)(device_keys)
    return chosen.reshape(N_COL, N_ROW, SLOTS).astype(jnp.int32)


def draw_tile_count(key, part):
    key = jax.random.fold_in(key, 12)
    level = jax.random.randint(key, (N_COL * N_ROW,), 0, 64)
    lowest = SLOTS // 5
    counts = lowest + (SLOTS - lowest) * level * level // 4096
    counts = jnp.maximum(counts, 1)
    busiest = jax.random.randint(jax.random.fold_in(key, 1), (), 0, N_COL * N_ROW)
    counts = jnp.where(jnp.arange(N_COL * N_ROW) == busiest, SLOTS, counts)
    return counts.reshape(N_COL, N_ROW).astype(jnp.int32)


def touch_ends(drawn, key, smallest, high):
    shape = drawn.shape
    place = [jax.random.randint(jax.random.fold_in(key, axis), (), 0, shape[axis]) for axis in range(len(shape))]
    drawn = drawn.at[tuple(place)].set(smallest)
    longest = shape.index(max(shape))
    place[longest] = (place[longest] + 1) % shape[longest]
    return drawn.at[tuple(place)].set(high)


def shard_levels(rng, extent, cuts, low, top_value):
    gain = 1.0
    for position, shards_of in cuts:
        draws = jax.random.uniform(jax.random.fold_in(jax.random.fold_in(rng, 6), position), (shards_of,), jnp.float32, low / len(cuts), top_value / len(cuts))
        gain = gain * jnp.repeat(jnp.exp(draws), extent[position] // shards_of).reshape((-1,) + (1,) * (len(extent) - 1 - position))
    return gain


def gaussian(stream_key, dims, deviation, limit, cuts=(), dtype=jnp.bfloat16):
    values = deviation * jax.random.normal(stream_key, dims, jnp.float32)
    if cuts:
        values = values * shard_levels(stream_key, dims, cuts, -0.22, 0.18)
    return jnp.clip(values, -limit, limit).astype(dtype)


def setup_inputs(seed: int = 0) -> dict:
    key_of = jax.random.split(jax.random.key(seed), 8)
    return {
        "out_grad": gaussian(key_of[0], (NODES, F), 1.0, 6.0, ((0, 512),)),
        "relu_mask": touch_ends((jax.random.randint(key_of[1], (NODES, F), 0, 2) < 1).astype(jnp.int32), jax.random.fold_in(key_of[1], 1), 0, 1),
        "features": gaussian(key_of[2], (NODES, F), (NODES ** -0.5), 0.0390625, ((0, 512),)),
        "weight": gaussian(key_of[3], (F, F), F ** -0.5, 0.375),
        "tile_values": gaussian(key_of[4], (N_COL, N_ROW, SLOTS, BLK, BLK), ((BLK * SLOTS) ** -0.5), 0.125, ((0, 16), (1, 32))),
        "tile_index": draw_tile_index(jax.random.fold_in(key_of[7], 71), 0),
        "tile_count": draw_tile_count(jax.random.fold_in(key_of[7], 71), 0),
    }


def device_part(stripe_blocks, tile_block, index_list, live_count):
    row_block = index_list // COLB
    col_block = index_list % COLB
    target = jnp.where(jnp.arange(SLOTS) < live_count, col_block, COLB).astype(jnp.int32)
    chosen = stripe_blocks[row_block]
    products = jnp.einsum('kab,kaf->kbf', tile_block.astype(jnp.float32), chosen.astype(jnp.float32))
    return jnp.zeros((COLB, BLK, F), jnp.float32).at[target].add(products, mode="drop")


def reference(out_grad, relu_mask, features, weight, tile_values, tile_index, tile_count):
    gradient = (out_grad.astype(jnp.float32) * relu_mask.astype(jnp.float32)).astype(jnp.bfloat16)
    blocks = gradient.reshape(N_COL, STRIPE, BLK, F)

    def per_stripe(total, inputs):
        stripe_blocks, stripe_tiles, stripe_index, stripe_count = inputs

        def one_device(device_inputs):
            return device_part(stripe_blocks, device_inputs[0], device_inputs[1], device_inputs[2])

        parts = lax.map(one_device, (stripe_tiles, stripe_index, stripe_count))
        parts = parts.reshape(N_ROW, N_COL, SEGB, BLK, F).transpose(1, 0, 2, 3, 4).reshape(NODES, F)
        return total + parts, None

    total, unused = lax.scan(per_stripe, jnp.zeros((NODES, F), jnp.float32), (blocks, tile_values, tile_index, tile_count))
    node_grad = total.astype(jnp.bfloat16)
    input_grad = jnp.einsum('no,io->ni', node_grad.astype(jnp.float32), weight.astype(jnp.float32)).astype(jnp.bfloat16)
    weight_grad = jnp.einsum('ni,no->io', features.astype(jnp.float32), node_grad.astype(jnp.float32))
    return input_grad, weight_grad
```

```python
import jax
import jax.numpy as jnp
from jax import lax
from jax.experimental import pallas as pl
from jax.experimental.pallas import tpu as pltpu
from jax.sharding import PartitionSpec as P

MESH = pl.DeviceIdType.MESH
BLK = 128
F = 256
SLOTS = 96
N_COL = 16
N_ROW = 32
COLB = 32
STRIPE = 64
HALF = N_COL // 2
GROUP = 4
PIECES = 4
PIECE = F // PIECES
SIGN = (1, -1)


def farthest(e, way):
    return HALF if way == e % 2 else HALF - 1


def loop(begin, end, f):
    def one(i, _):
        f(i)
        return 0
    lax.fori_loop(begin, end, one, 0)


def kernel(
    count, index_hbm, grad_hbm, mask_hbm, feat_hbm, weight_hbm, tiles_hbm,
    input_out, weight_out,
    index_ref, meta_v, meta, grad_ref, mask_ref, feats, weight_ref, tiles, stripe_0, stripe_1, parts,
    sums_out, sums_in, node_t, total, dw, plane_in, line, done,
    load_sem, meta_sem, g_send, g_recv, f_send, f_recv, s_send, s_recv,
    a_send, a_recv, z_send, z_recv, b_send, b_recv,
):
    c = lax.axis_index("col")
    r = lax.axis_index("row")
    x, y, k = lax.div(r, 8), lax.rem(lax.div(r, 2), 4), lax.rem(r, 2)
    stripe = (stripe_0, stripe_1)

    def col(d):
        return lax.rem(c + d + N_COL, N_COL)

    def row(d):
        return lax.rem(r + d, N_ROW)

    def copy(src, dst, send, recv, device):
        return pltpu.make_async_remote_copy(
            src_ref=src, dst_ref=dst, send_sem=send, recv_sem=recv,
            device_id=device, device_id_type=MESH,
        )

    fetches = [
        pltpu.make_async_copy(source, target, load_sem.at[i])
        for i, (source, target) in enumerate((
            (grad_hbm, grad_ref), (mask_hbm, mask_ref), (index_hbm, index_ref),
            (feat_hbm, feats.at[c]), (weight_hbm, weight_ref), (tiles_hbm, tiles),
        ))
    ]
    for fetch in fetches:
        fetch.start()

    barrier = pltpu.get_barrier_semaphore()
    loop(1, N_COL, lambda d: pl.semaphore_signal(barrier, inc=1, device_id=(col(d), r), device_id_type=MESH))
    loop(1, N_ROW, lambda d: pl.semaphore_signal(barrier, inc=1, device_id=(c, row(d)), device_id_type=MESH))

    fetches[0].wait()
    fetches[1].wait()
    grad = grad_ref[...].astype(jnp.float32) * mask_ref[...].astype(jnp.float32)
    grad_t = jnp.transpose(grad).astype(jnp.bfloat16)
    for h in range(2):
        for e in range(2):
            stripe[h][2 * r + e] = grad_t[h * BLK:(h + 1) * BLK, e * BLK:(e + 1) * BLK]
        parts[h, SLOTS] = jnp.zeros((BLK, BLK), jnp.float32)
    fetches[2].wait()
    fetches[3].wait()

    pl.semaphore_wait(barrier, N_ROW - 1 + N_COL - 1)

    def peer(a, b):
        dx = a * (1 - k) + b * k
        dy = a * k + b * (1 - k)
        return (lax.rem(x + dx, 4) * 4 + lax.rem(y + dy, 4)) * 2 + k

    sibling = r + 1 - 2 * k

    def unit(h, at):
        return stripe[h].at[pl.ds(2 * at, 2)]

    def push(h, at, target, number):
        copy(unit(h, at), unit(h, at), g_send.at[h, number], g_recv.at[h, at], (c, target)).start()

    def arrived(h, at):
        copy(unit(h, at), unit(h, at), g_send.at[h, 0], g_recv.at[h, at], (c, sibling)).wait_recv()

    order = (1, 3, 2)

    def gather_start(h):
        for i, a in enumerate(order):
            push(h, r, peer(a, 0), i)
        for i, b in enumerate(order):
            push(h, r, peer(0, b), 3 + i)
        push(h, r, sibling, 6)

    def gather_first(h):
        for i, a in enumerate(order):
            at = peer(4 - a, 0)
            arrived(h, at)
            for j, b in enumerate(order):
                push(h, at, peer(0, b), 7 + 4 * i + j)
            push(h, at, sibling, 7 + 4 * i + 3)

    def gather_second(h, j):
        for i, a in enumerate((0,) + order):
            at = peer((4 - a) % 4, 4 - order[j])
            arrived(h, at)
            push(h, at, sibling, 19 + 4 * j + i)

    def gather_end(h):
        loop(0, N_ROW // 2, lambda i: arrived(h, 2 * i + 1 - k))

    def gather_sent(h):
        loop(0, 31, lambda i: copy(
            unit(h, r), unit(h, r), g_send.at[h, i], g_recv.at[h, r], (c, sibling)).wait_send())

    def feature(q, way, far):
        origin = col(-SIGN[way] * far)
        held = feats.at[origin, pl.ds(q * PIECE, PIECE)]
        return copy(held, held, f_send.at[q, way, far], f_recv.at[q, origin], (col(SIGN[way]), r))

    def feature_step(far):
        for q in range(PIECES):
            for way in range(2):
                if far < farthest(q, way):
                    if far > 0:
                        feature(q, way, far).wait_recv()
                    feature(q, way, far).start()

    def feature_end():
        for q in range(PIECES):
            for way in range(2):
                feature(q, way, farthest(q, way)).wait_recv()

    def feature_sent():
        for q in range(PIECES):
            for way in range(2):
                loop(0, farthest(q, way), lambda far: feature(q, way, far).wait_send())

    def positions():
        index = index_ref[...]
        down = lax.broadcasted_iota(jnp.int32, (SLOTS, SLOTS), 0)
        across = lax.broadcasted_iota(jnp.int32, (SLOTS, SLOTS), 1)
        column = jnp.broadcast_to(lax.rem(index, COLB), (SLOTS, SLOTS))
        column_down = jnp.sum(jnp.where(down == across, column, 0), axis=1, keepdims=True)
        column_down = jnp.broadcast_to(column_down, (SLOTS, SLOTS))
        previous = jnp.max(
            jnp.where((column == column_down) & (down < across), down, -1), axis=0, keepdims=True
        )
        last = jnp.max(
            jnp.where((column_down == across) & (down < count[0, 0]), down, -1), axis=0, keepdims=True
        )
        meta_v[...] = jnp.zeros_like(meta_v)
        meta_v[0:1, 0:SLOTS] = lax.div(index, COLB)
        meta_v[1:2, 0:SLOTS] = jnp.where(previous < 0, SLOTS, previous)
        meta_v[2:3, 0:SLOTS] = jnp.where(last < 0, SLOTS, last)
        pltpu.make_async_copy(meta_v, meta, meta_sem).start()

    def products(h, begin=0, end=SLOTS):
        def some(i):
            for j in range(GROUP):
                n = i * GROUP + j
                got = jnp.dot(stripe[h][meta[0, n]], tiles[n], preferred_element_type=jnp.float32)
                parts[h, n] = got + parts[h, meta[1, n]]
        loop(begin // GROUP, end // GROUP, some)

    def own(h, s, e):
        return parts[h, meta[2, 2 * s + e]]

    def message(h, e, way, far):
        slot = (h, e, way, far - 1)
        return copy(
            sums_out.at[slot], sums_in.at[slot], s_send.at[slot], s_recv.at[slot], (col(SIGN[way]), r)
        )

    def received(h, e, way, far):
        message(h, e, way, far).wait_recv()
        return sums_in[h, e, way, far - 1].astype(jnp.float32)

    def chain(h, far):
        for e in range(2):
            for way in range(2):
                most = farthest(e, way)
                if far <= most:
                    value = own(h, col(SIGN[way] * far), e)
                    if far < most:
                        value = value + received(h, e, way, far + 1)
                    sums_out[h, e, way, far - 1] = value.astype(jnp.bfloat16)
                    message(h, e, way, far).start()

    def finish(h):
        for e in range(2):
            value = own(h, c, e)
            for way in range(2):
                value = value + received(h, e, way, 1)
            node_t[h * BLK:(h + 1) * BLK, e * BLK:(e + 1) * BLK] = value

    def sums_sent(h):
        for e in range(2):
            for way in range(2):
                loop(1, farthest(e, way) + 1, lambda far: message(h, e, way, far).wait_send())

    def weight_term(begin, end):
        if begin == 0:
            total[...] = jnp.zeros_like(total)

        def one(s):
            terms = jnp.concatenate([
                jnp.concatenate([own(h, s, e).astype(jnp.bfloat16) for e in range(2)], axis=1)
                for h in range(2)
            ], axis=0)
            total[...] += jnp.dot(terms, feats[s], preferred_element_type=jnp.float32)

        loop(begin, end, one)
        if end == N_COL:
            dw[...] = total[...].reshape(N_ROW, F // N_ROW, F)

    def term(at):
        return copy(dw.at[at], plane_in.at[r], a_send.at[at], a_recv.at[r], (c, at))

    def term_from(at):
        return copy(dw.at[at], plane_in.at[at], a_send.at[at], a_recv.at[at], (c, at))

    def along(at):
        return copy(line.at[c], line.at[c], z_send.at[at], z_recv.at[c], (at, r))

    def along_from(at):
        return copy(line.at[at], line.at[at], z_send.at[at], z_recv.at[at], (at, r))

    def back(at):
        return copy(done.at[r], done.at[r], b_send.at[at], b_recv.at[r], (c, at))

    def back_from(at):
        return copy(done.at[at], done.at[at], b_send.at[at], b_recv.at[at], (c, at))

    def share_plane():
        loop(1, N_ROW, lambda d: term(row(d)).start())
        plane_in[r] = dw[r]

    def share_line():
        loop(1, N_ROW, lambda d: term_from(row(d)).wait_recv())
        mine = jnp.sum(plane_in[...], axis=0)
        mine = jnp.concatenate([mine[:, :BLK], mine[:, BLK:]], axis=0)
        line[c] = mine.astype(jnp.bfloat16)
        loop(1, N_COL, lambda d: along(col(d)).start())

    def share_back():
        loop(1, N_COL, lambda d: along_from(col(d)).wait_recv())
        whole = jnp.sum(line[...].astype(jnp.float32), axis=0)
        done[r] = jnp.concatenate([whole[:F // N_ROW], whole[F // N_ROW:]], axis=1)
        loop(1, N_ROW, lambda d: back(row(d)).start())

    gather_start(0)
    feature_step(0)
    gather_start(1)
    positions()
    gather_first(0)
    feature_step(1)
    gather_first(1)
    feature_step(2)
    gather_second(0, 0)
    feature_step(3)
    gather_second(0, 1)
    gather_second(0, 2)
    feature_step(4)
    gather_second(1, 0)
    gather_second(1, 1)
    feature_step(5)
    gather_second(1, 2)
    fetches[4].wait()
    fetches[5].wait()
    pltpu.make_async_copy(meta_v, meta, meta_sem).wait()
    gather_end(0)
    feature_step(6)
    products(0, 0, SLOTS // 2)
    feature_step(7)
    products(0, SLOTS // 2, SLOTS)
    chain(0, 8)
    gather_end(1)
    products(1, 0, SLOTS // 2)
    chain(0, 7)
    products(1, SLOTS // 2, SLOTS)
    chain(1, 8)
    chain(0, 6)
    feature_end()
    weight_term(0, N_COL // 2)
    chain(1, 7)
    chain(0, 5)
    weight_term(N_COL // 2, N_COL)
    share_plane()
    chain(1, 6)
    chain(0, 4)
    gather_sent(0)
    gather_sent(1)
    chain(1, 5)
    chain(0, 3)
    share_line()
    chain(1, 4)
    chain(0, 2)
    feature_sent()
    chain(1, 3)
    chain(0, 1)
    chain(1, 2)
    finish(0)
    chain(1, 1)
    sums_sent(0)
    share_back()
    finish(1)
    node = jnp.transpose(node_t[...])
    high = node.astype(jnp.bfloat16)
    low = (node - high.astype(jnp.float32)).astype(jnp.bfloat16)
    input_out[...] = sum(
        lax.dot_general(half, weight_ref[...], (((1,), (1,)), ((), ())), preferred_element_type=jnp.float32)
        for half in (high, low)
    ).astype(jnp.bfloat16)
    sums_sent(1)
    loop(1, N_ROW, lambda d: term(row(d)).wait_send())
    loop(1, N_COL, lambda d: along(col(d)).wait_send())
    loop(1, N_ROW, lambda d: back_from(row(d)).wait_recv())
    weight_out[...] = done[...].reshape(F, F)
    loop(1, N_ROW, lambda d: back(row(d)).wait_send())


def on_device(out_grad, relu_mask, features, weight, tile_values, tile_index, tile_count):
    vmem = pl.BlockSpec(memory_space=pltpu.VMEM)
    anywhere = pl.BlockSpec(memory_space=pl.ANY)
    dma = pltpu.SemaphoreType.DMA
    bf16, f32, i32 = jnp.bfloat16, jnp.float32, jnp.int32
    input_grad, weight_t = pl.pallas_call(
        kernel,
        name="layer_backward",
        out_shape=(jax.ShapeDtypeStruct((F, F), bf16), jax.ShapeDtypeStruct((F, F), f32)),
        in_specs=[pl.BlockSpec(memory_space=pltpu.SMEM)] + [anywhere] * 6,
        out_specs=(vmem, vmem),
        scratch_shapes=[
            pltpu.VMEM((1, SLOTS), i32),
            pltpu.VMEM((8, BLK), i32),
            pltpu.SMEM((8, BLK), i32),
            pltpu.VMEM((F, F), bf16),
            pltpu.VMEM((F, F), i32),
            pltpu.VMEM((N_COL, F, F), bf16),
            pltpu.VMEM((F, F), bf16),
            pltpu.VMEM((SLOTS, BLK, BLK), bf16),
            pltpu.VMEM((STRIPE, BLK, BLK), bf16),
            pltpu.VMEM((STRIPE, BLK, BLK), bf16),
            pltpu.VMEM((2, SLOTS + 1, BLK, BLK), f32),
            pltpu.VMEM((2, 2, 2, HALF, BLK, BLK), bf16),
            pltpu.VMEM((2, 2, 2, HALF, BLK, BLK), bf16),
            pltpu.VMEM((F, F), f32),
            pltpu.VMEM((F, F), f32),
            pltpu.VMEM((N_ROW, F // N_ROW, F), f32),
            pltpu.VMEM((N_ROW, F // N_ROW, F), f32),
            pltpu.VMEM((N_COL, 2 * F // N_ROW, BLK), bf16),
            pltpu.VMEM((N_ROW, F // N_ROW, F), f32),
            dma((6,)), dma, dma((2, 31)), dma((2, N_ROW)), dma((PIECES, 2, HALF)), dma((PIECES, N_COL)),
            dma((2, 2, 2, HALF)), dma((2, 2, 2, HALF)),
            dma((N_ROW,)), dma((N_ROW,)), dma((N_COL,)), dma((N_COL,)), dma((N_ROW,)), dma((N_ROW,)),
        ],
        compiler_params=pltpu.CompilerParams(
            collective_id=0, has_side_effects=True, vmem_limit_bytes=60 * 2**20
        ),
        cost_estimate=pl.CostEstimate(flops=2 * 10**9, bytes_accessed=8 * 2**20, transcendentals=0),
    )(
        tile_count, tile_index.reshape(1, SLOTS), out_grad, relu_mask, features, weight,
        tile_values.reshape(SLOTS, BLK, BLK),
    )
    return input_grad, weight_t.T


def solution(mesh):
    placed = (
        P(("col", "row"), None),
        P(("col", "row"), None),
        P(("col", "row"), None),
        P(),
        P("col", "row", None, None, None),
        P("col", "row", None),
        P("col", "row"),
    )
    return jax.shard_map(
        on_device,
        mesh=mesh,
        in_specs=placed,
        out_specs=(P(("col", "row"), None), P()),
        check_vma=False,
    )
```

```python
import jax
import jax.numpy as jnp
from jax import lax
from jax.experimental import pallas as pl
from jax.experimental.pallas import tpu as pltpu
from jax.sharding import PartitionSpec as P

MESH = pl.DeviceIdType.MESH
BLK = 128
F = 256
SLOTS = 96
N_COL = 16
N_ROW = 32
COLB = 32
STRIPE = 64
HALF = N_COL // 2
GROUP = 8
PIECES = 4
PIECE = F // PIECES
RADIUS = 7
SIGN = (1, -1)


def farthest(e, way):
    return HALF if way == e % 2 else HALF - 1


def loop(begin, end, f):
    def one(i, _):
        f(i)
        return 0
    lax.fori_loop(begin, end, one, 0)


def kernel(
    count, index_hbm, grad_hbm, mask_hbm, feat_hbm, weight_hbm, tiles_hbm,
    input_out, weight_out,
    index_ref, meta_v, meta, grad_ref, mask_ref, feats, weight_ref, tiles, stripe_0, stripe_1, parts,
    sums_out, sums_in, node_t, total, dw, plane_in, line, done,
    load_sem, meta_sem, g_send, g_recv, f_send, f_recv, s_send, s_recv,
    a_send, a_recv, z_send, z_recv, b_send, b_recv,
):
    c = lax.axis_index("col")
    r = lax.axis_index("row")
    x, y, k = lax.div(r, 8), lax.rem(lax.div(r, 2), 4), lax.rem(r, 2)
    stripe = (stripe_0, stripe_1)

    def col(d):
        return lax.rem(c + d + N_COL, N_COL)

    def row(d):
        return lax.rem(r + d, N_ROW)

    def copy(src, dst, send, recv, device):
        return pltpu.make_async_remote_copy(
            src_ref=src, dst_ref=dst, send_sem=send, recv_sem=recv,
            device_id=device, device_id_type=MESH,
        )

    fetches = [
        pltpu.make_async_copy(source, target, load_sem.at[i])
        for i, (source, target) in enumerate((
            (grad_hbm, grad_ref), (mask_hbm, mask_ref), (index_hbm, index_ref),
            (feat_hbm, feats.at[c]), (weight_hbm, weight_ref), (tiles_hbm, tiles),
        ))
    ]
    for fetch in fetches:
        fetch.start()

    barrier = pltpu.get_barrier_semaphore()
    loop(1, N_COL, lambda d: pl.semaphore_signal(barrier, inc=1, device_id=(col(d), r), device_id_type=MESH))
    loop(1, N_ROW, lambda d: pl.semaphore_signal(barrier, inc=1, device_id=(c, row(d)), device_id_type=MESH))

    fetches[0].wait()
    fetches[1].wait()
    grad = grad_ref[...].astype(jnp.float32) * mask_ref[...].astype(jnp.float32)
    grad_t = jnp.transpose(grad).astype(jnp.bfloat16)
    for h in range(2):
        for e in range(2):
            stripe[h][2 * r + e] = grad_t[h * BLK:(h + 1) * BLK, e * BLK:(e + 1) * BLK]
        parts[h, SLOTS] = jnp.zeros((BLK, BLK), jnp.float32)
    fetches[2].wait()
    fetches[3].wait()

    pl.semaphore_wait(barrier, N_ROW - 1 + N_COL - 1)

    def peer(a, b):
        dx = a * (1 - k) + b * k
        dy = a * k + b * (1 - k)
        return (lax.rem(x + dx, 4) * 4 + lax.rem(y + dy, 4)) * 2 + k

    sibling = r + 1 - 2 * k

    def unit(h, at):
        return stripe[h].at[pl.ds(2 * at, 2)]

    def push(h, at, target, number):
        copy(unit(h, at), unit(h, at), g_send.at[h, number], g_recv.at[h, at], (c, target)).start()

    def arrived(h, at):
        copy(unit(h, at), unit(h, at), g_send.at[h, 0], g_recv.at[h, at], (c, sibling)).wait_recv()

    order = (1, 3, 2)

    def gather_start(h):
        for i, a in enumerate(order):
            push(h, r, peer(a, 0), i)
        for i, b in enumerate(order):
            push(h, r, peer(0, b), 3 + i)
        push(h, r, sibling, 6)

    def gather_first(h):
        for i, a in enumerate(order):
            at = peer(4 - a, 0)
            arrived(h, at)
            for j, b in enumerate(order):
                push(h, at, peer(0, b), 7 + 4 * i + j)
            push(h, at, sibling, 7 + 4 * i + 3)

    def gather_second(h, j):
        for i, a in enumerate((0,) + order):
            at = peer((4 - a) % 4, 4 - order[j])
            arrived(h, at)
            push(h, at, sibling, 19 + 4 * j + i)

    def gather_end(h):
        loop(0, N_ROW // 2, lambda i: arrived(h, 2 * i + 1 - k))

    def gather_sent(h):
        loop(0, 31, lambda i: copy(
            unit(h, r), unit(h, r), g_send.at[h, i], g_recv.at[h, r], (c, sibling)).wait_send())

    def feature(q, way, far):
        origin = col(-SIGN[way] * far)
        held = feats.at[origin, pl.ds(q * PIECE, PIECE)]
        return copy(held, held, f_send.at[q, way, far], f_recv.at[q, origin], (col(SIGN[way]), r))

    def feature_step(far):
        for q in range(PIECES):
            for way in range(2):
                if far > 0:
                    feature(q, way, far).wait_recv()
                feature(q, way, far).start()

    def feature_end():
        for q in range(PIECES):
            for way in range(2):
                feature(q, way, RADIUS).wait_recv()

    def feature_sent():
        for q in range(PIECES):
            for way in range(2):
                loop(0, RADIUS, lambda far: feature(q, way, far).wait_send())

    def positions():
        index = index_ref[...]
        down = lax.broadcasted_iota(jnp.int32, (SLOTS, SLOTS), 0)
        across = lax.broadcasted_iota(jnp.int32, (SLOTS, SLOTS), 1)
        column = jnp.broadcast_to(lax.rem(index, COLB), (SLOTS, SLOTS))
        column_down = jnp.sum(jnp.where(down == across, column, 0), axis=1, keepdims=True)
        column_down = jnp.broadcast_to(column_down, (SLOTS, SLOTS))
        previous = jnp.max(
            jnp.where((column == column_down) & (down < across), down, -1), axis=0, keepdims=True
        )
        last = jnp.max(
            jnp.where((column_down == across) & (down < count[0, 0]), down, -1), axis=0, keepdims=True
        )
        meta_v[...] = jnp.zeros_like(meta_v)
        meta_v[0:1, 0:SLOTS] = lax.div(index, COLB)
        meta_v[1:2, 0:SLOTS] = jnp.where(previous < 0, SLOTS, previous)
        meta_v[2:3, 0:SLOTS] = jnp.where(last < 0, SLOTS, last)
        pltpu.make_async_copy(meta_v, meta, meta_sem).start()

    def products(h, begin=0, end=SLOTS):
        def some(i):
            for j in range(GROUP):
                n = i * GROUP + j
                got = jnp.dot(stripe[h][meta[0, n]], tiles[n], preferred_element_type=jnp.float32)
                parts[h, n] = got + parts[h, meta[1, n]]
        loop(begin // GROUP, end // GROUP, some)

    def own(h, s, e):
        return parts[h, meta[2, 2 * s + e]]

    def message(h, e, way, far):
        slot = (h, e, way, far - 1)
        return copy(
            sums_out.at[slot], sums_in.at[slot], s_send.at[slot], s_recv.at[slot], (col(SIGN[way]), r)
        )

    def received(h, e, way, far):
        message(h, e, way, far).wait_recv()
        return sums_in[h, e, way, far - 1].astype(jnp.float32)

    def chain(h, far):
        for e in range(2):
            for way in range(2):
                most = farthest(e, way)
                if far <= most:
                    value = own(h, col(SIGN[way] * far), e)
                    if far < most:
                        value = value + received(h, e, way, far + 1)
                    sums_out[h, e, way, far - 1] = value.astype(jnp.bfloat16)
                    message(h, e, way, far).start()

    def finish(h):
        for e in range(2):
            value = own(h, c, e)
            for way in range(2):
                value = value + received(h, e, way, 1)
            node_t[h * BLK:(h + 1) * BLK, e * BLK:(e + 1) * BLK] = value

    def sums_sent(h):
        for e in range(2):
            for way in range(2):
                loop(1, farthest(e, way) + 1, lambda far: message(h, e, way, far).wait_send())

    def joined(part):
        return jnp.concatenate([
            jnp.concatenate([part(h, e).astype(jnp.bfloat16) for e in range(2)], axis=1) for h in range(2)
        ], axis=0)

    def weight_near():
        def at(s):
            terms = joined(lambda h, e: own(h, s, e))
            return jnp.dot(terms, feats[s], preferred_element_type=jnp.float32)

        total[...] = at(c)

        def both(j):
            total[...] += at(col(j)) + at(col(-j))

        loop(1, RADIUS, both)

    def weight_far():
        got = total[...]
        for way in range(2):
            terms = joined(lambda h, e: sums_out[h, e, way, RADIUS - 1])
            got = got + jnp.dot(terms, feats[col(SIGN[way] * RADIUS)], preferred_element_type=jnp.float32)
        dw[...] = got.reshape(N_ROW, F // N_ROW, F)

    def term(at):
        return copy(dw.at[at], plane_in.at[r], a_send.at[at], a_recv.at[r], (c, at))

    def term_from(at):
        return copy(dw.at[at], plane_in.at[at], a_send.at[at], a_recv.at[at], (c, at))

    def along(at):
        return copy(line.at[c], line.at[c], z_send.at[at], z_recv.at[c], (at, r))

    def along_from(at):
        return copy(line.at[at], line.at[at], z_send.at[at], z_recv.at[at], (at, r))

    def back(at):
        return copy(done.at[r], done.at[r], b_send.at[at], b_recv.at[r], (c, at))

    def back_from(at):
        return copy(done.at[at], done.at[at], b_send.at[at], b_recv.at[at], (c, at))

    def share_plane():
        loop(1, N_ROW, lambda d: term(row(d)).start())
        plane_in[r] = dw[r]

    def share_line():
        loop(1, N_ROW, lambda d: term_from(row(d)).wait_recv())
        mine = jnp.sum(plane_in[...], axis=0)
        mine = jnp.concatenate([mine[:, :BLK], mine[:, BLK:]], axis=0)
        line[c] = mine.astype(jnp.bfloat16)
        loop(1, N_COL, lambda d: along(col(d)).start())

    def share_back():
        loop(1, N_COL, lambda d: along_from(col(d)).wait_recv())
        whole = jnp.sum(line[...].astype(jnp.float32), axis=0)
        done[r] = jnp.concatenate([whole[:F // N_ROW], whole[F // N_ROW:]], axis=1)
        loop(1, N_ROW, lambda d: back(row(d)).start())

    gather_start(0)
    feature_step(0)
    positions()
    feature_step(1)
    gather_first(0)
    gather_start(1)
    feature_step(2)
    gather_second(0, 0)
    feature_step(3)
    gather_first(1)
    gather_second(0, 1)
    gather_second(0, 2)
    feature_step(4)
    fetches[4].wait()
    fetches[5].wait()
    pltpu.make_async_copy(meta_v, meta, meta_sem).wait()
    gather_end(0)
    products(0, 0, SLOTS // 2)
    feature_step(5)
    gather_second(1, 0)
    gather_second(1, 1)
    products(0, SLOTS // 2, SLOTS)
    chain(0, 8)
    feature_step(6)
    gather_second(1, 2)
    gather_end(1)
    products(1, 0, SLOTS // 2)
    chain(0, 7)
    products(1, SLOTS // 2, SLOTS)
    chain(1, 8)
    feature_end()
    weight_near()
    chain(0, 6)
    chain(1, 7)
    weight_far()
    share_plane()
    chain(0, 5)
    chain(1, 6)
    gather_sent(0)
    chain(0, 4)
    chain(1, 5)
    share_line()
    gather_sent(1)
    chain(0, 3)
    chain(1, 4)
    feature_sent()
    chain(0, 2)
    chain(1, 3)
    chain(0, 1)
    chain(1, 2)
    share_back()
    finish(0)
    chain(1, 1)
    sums_sent(0)
    finish(1)
    node = jnp.transpose(node_t[...])
    high = node.astype(jnp.bfloat16)
    low = (node - high.astype(jnp.float32)).astype(jnp.bfloat16)
    input_out[...] = sum(
        lax.dot_general(half, weight_ref[...], (((1,), (1,)), ((), ())), preferred_element_type=jnp.float32)
        for half in (high, low)
    ).astype(jnp.bfloat16)
    sums_sent(1)
    loop(1, N_ROW, lambda d: term(row(d)).wait_send())
    loop(1, N_COL, lambda d: along(col(d)).wait_send())
    loop(1, N_ROW, lambda d: back_from(row(d)).wait_recv())
    weight_out[...] = done[...].reshape(F, F)
    loop(1, N_ROW, lambda d: back(row(d)).wait_send())


def on_device(out_grad, relu_mask, features, weight, tile_values, tile_index, tile_count):
    vmem = pl.BlockSpec(memory_space=pltpu.VMEM)
    anywhere = pl.BlockSpec(memory_space=pl.ANY)
    dma = pltpu.SemaphoreType.DMA
    bf16, f32, i32 = jnp.bfloat16, jnp.float32, jnp.int32
    input_grad, weight_t = pl.pallas_call(
        kernel,
        name="layer_backward",
        out_shape=(jax.ShapeDtypeStruct((F, F), bf16), jax.ShapeDtypeStruct((F, F), f32)),
        in_specs=[pl.BlockSpec(memory_space=pltpu.SMEM)] + [anywhere] * 6,
        out_specs=(vmem, vmem),
        scratch_shapes=[
            pltpu.VMEM((1, SLOTS), i32),
            pltpu.VMEM((8, BLK), i32),
            pltpu.SMEM((8, BLK), i32),
            pltpu.VMEM((F, F), bf16),
            pltpu.VMEM((F, F), i32),
            pltpu.VMEM((N_COL, F, F), bf16),
            pltpu.VMEM((F, F), bf16),
            pltpu.VMEM((SLOTS, BLK, BLK), bf16),
            pltpu.VMEM((STRIPE, BLK, BLK), bf16),
            pltpu.VMEM((STRIPE, BLK, BLK), bf16),
            pltpu.VMEM((2, SLOTS + 1, BLK, BLK), f32),
            pltpu.VMEM((2, 2, 2, HALF, BLK, BLK), bf16),
            pltpu.VMEM((2, 2, 2, HALF, BLK, BLK), bf16),
            pltpu.VMEM((F, F), f32),
            pltpu.VMEM((F, F), f32),
            pltpu.VMEM((N_ROW, F // N_ROW, F), f32),
            pltpu.VMEM((N_ROW, F // N_ROW, F), f32),
            pltpu.VMEM((N_COL, 2 * F // N_ROW, BLK), bf16),
            pltpu.VMEM((N_ROW, F // N_ROW, F), f32),
            dma((6,)), dma, dma((2, 31)), dma((2, N_ROW)), dma((PIECES, 2, RADIUS)), dma((PIECES, N_COL)),
            dma((2, 2, 2, HALF)), dma((2, 2, 2, HALF)),
            dma((N_ROW,)), dma((N_ROW,)), dma((N_COL,)), dma((N_COL,)), dma((N_ROW,)), dma((N_ROW,)),
        ],
        compiler_params=pltpu.CompilerParams(
            collective_id=0, has_side_effects=True, vmem_limit_bytes=60 * 2**20
        ),
        cost_estimate=pl.CostEstimate(flops=2 * 10**9, bytes_accessed=8 * 2**20, transcendentals=0),
    )(
        tile_count, tile_index.reshape(1, SLOTS), out_grad, relu_mask, features, weight,
        tile_values.reshape(SLOTS, BLK, BLK),
    )
    return input_grad, weight_t.T


def solution(mesh):
    placed = (
        P(("col", "row"), None),
        P(("col", "row"), None),
        P(("col", "row"), None),
        P(),
        P("col", "row", None, None, None),
        P("col", "row", None),
        P("col", "row"),
    )
    return jax.shard_map(
        on_device,
        mesh=mesh,
        in_specs=placed,
        out_specs=(P(("col", "row"), None), P()),
        check_vma=False,
    )
```

```python
import jax
import jax.numpy as jnp
from jax import lax
from jax.experimental import pallas as pl
from jax.experimental.pallas import tpu as pltpu
from jax.sharding import PartitionSpec as P

MESH = pl.DeviceIdType.MESH
BLK = 128
F = 256
SLOTS = 96
N_COL = 16
N_ROW = 32
COLB = 32
STRIPE = 64
HALF = N_COL // 2
GROUP = 16
PIECES = 4
PIECE = F // PIECES
RADIUS = 7
JOINS = (2,)
SIGN = (1, -1)


def farthest(e, way):
    return HALF if way == e % 2 else HALF - 1


def loop(begin, end, f):
    def one(i, _):
        f(i)
        return 0
    lax.fori_loop(begin, end, one, 0)


def kernel(
    count, index_hbm, grad_hbm, mask_hbm, feat_hbm, weight_hbm, tiles_hbm,
    input_out, weight_out,
    index_ref, meta_v, meta, grad_ref, mask_ref, feats, weight_ref, tiles, stripe_0, stripe_1, parts,
    sums_out, sums_in, node_t, total, dw, plane_in, line, done,
    load_sem, meta_sem, g_send, g_recv, f_send, f_recv, s_send, s_recv,
    a_send, a_recv, z_send, z_recv, b_send, b_recv,
):
    c = lax.axis_index("col")
    r = lax.axis_index("row")
    x, y, k = lax.div(r, 8), lax.rem(lax.div(r, 2), 4), lax.rem(r, 2)
    stripe = (stripe_0, stripe_1)

    def col(d):
        return lax.rem(c + d + N_COL, N_COL)

    def row(d):
        return lax.rem(r + d, N_ROW)

    def copy(src, dst, send, recv, device):
        return pltpu.make_async_remote_copy(
            src_ref=src, dst_ref=dst, send_sem=send, recv_sem=recv,
            device_id=device, device_id_type=MESH,
        )

    fetches = [
        pltpu.make_async_copy(source, target, load_sem.at[i])
        for i, (source, target) in enumerate((
            (grad_hbm, grad_ref), (mask_hbm, mask_ref), (index_hbm, index_ref),
            (feat_hbm, feats.at[c]), (weight_hbm, weight_ref), (tiles_hbm, tiles),
        ))
    ]
    for fetch in fetches:
        fetch.start()

    barrier = pltpu.get_barrier_semaphore()
    loop(1, N_COL, lambda d: pl.semaphore_signal(barrier, inc=1, device_id=(col(d), r), device_id_type=MESH))
    loop(1, N_ROW, lambda d: pl.semaphore_signal(barrier, inc=1, device_id=(c, row(d)), device_id_type=MESH))

    fetches[0].wait()
    fetches[1].wait()
    grad = grad_ref[...].astype(jnp.float32) * mask_ref[...].astype(jnp.float32)
    grad_t = jnp.transpose(grad).astype(jnp.bfloat16)
    for h in range(2):
        for e in range(2):
            stripe[h][2 * r + e] = grad_t[h * BLK:(h + 1) * BLK, e * BLK:(e + 1) * BLK]
        parts[h, SLOTS] = jnp.zeros((BLK, BLK), jnp.float32)
    fetches[2].wait()
    fetches[3].wait()

    pl.semaphore_wait(barrier, N_ROW - 1 + N_COL - 1)

    def peer(a, b):
        dx = a * (1 - k) + b * k
        dy = a * k + b * (1 - k)
        return (lax.rem(x + dx, 4) * 4 + lax.rem(y + dy, 4)) * 2 + k

    sibling = r + 1 - 2 * k

    def unit(h, at):
        return stripe[h].at[pl.ds(2 * at, 2)]

    def push(h, at, target, number):
        copy(unit(h, at), unit(h, at), g_send.at[h, number], g_recv.at[h, at], (c, target)).start()

    def arrived(h, at):
        copy(unit(h, at), unit(h, at), g_send.at[h, 0], g_recv.at[h, at], (c, sibling)).wait_recv()

    order = (1, 3, 2)

    def gather_start(h):
        for i, a in enumerate(order):
            push(h, r, peer(a, 0), i)
        for i, b in enumerate(order):
            push(h, r, peer(0, b), 3 + i)
        push(h, r, sibling, 6)

    def gather_first(h):
        for i, a in enumerate(order):
            at = peer(4 - a, 0)
            arrived(h, at)
            for j, b in enumerate(order):
                push(h, at, peer(0, b), 7 + 4 * i + j)
            push(h, at, sibling, 7 + 4 * i + 3)

    def gather_second(h, j):
        for i, a in enumerate((0,) + order):
            at = peer((4 - a) % 4, 4 - order[j])
            arrived(h, at)
            push(h, at, sibling, 19 + 4 * j + i)

    def gather_end(h):
        loop(0, N_ROW // 2, lambda i: arrived(h, 2 * i + 1 - k))

    def gather_sent(h):
        loop(0, 31, lambda i: copy(
            unit(h, r), unit(h, r), g_send.at[h, i], g_recv.at[h, r], (c, sibling)).wait_send())

    def feature(q, way, far):
        origin = col(-SIGN[way] * far)
        held = feats.at[origin, pl.ds(q * PIECE, PIECE)]
        return copy(held, held, f_send.at[q, way, far], f_recv.at[q, origin], (col(SIGN[way]), r))

    def feature_step(far):
        for q in range(PIECES):
            for way in range(2):
                if far > 0:
                    feature(q, way, far).wait_recv()
                feature(q, way, far).start()

    def feature_end():
        for q in range(PIECES):
            for way in range(2):
                feature(q, way, RADIUS).wait_recv()

    def feature_sent():
        for q in range(PIECES):
            for way in range(2):
                loop(0, RADIUS, lambda far: feature(q, way, far).wait_send())

    def positions():
        index = index_ref[...]
        down = lax.broadcasted_iota(jnp.int32, (SLOTS, SLOTS), 0)
        across = lax.broadcasted_iota(jnp.int32, (SLOTS, SLOTS), 1)
        column = jnp.broadcast_to(lax.rem(index, COLB), (SLOTS, SLOTS))
        column_down = jnp.sum(jnp.where(down == across, column, 0), axis=1, keepdims=True)
        column_down = jnp.broadcast_to(column_down, (SLOTS, SLOTS))
        previous = jnp.max(
            jnp.where((column == column_down) & (down < across), down, -1), axis=0, keepdims=True
        )
        last = jnp.max(
            jnp.where((column_down == across) & (down < count[0, 0]), down, -1), axis=0, keepdims=True
        )
        meta_v[...] = jnp.zeros_like(meta_v)
        meta_v[0:1, 0:SLOTS] = lax.div(index, COLB)
        meta_v[1:2, 0:SLOTS] = jnp.where(previous < 0, SLOTS, previous)
        meta_v[2:3, 0:SLOTS] = jnp.where(last < 0, SLOTS, last)
        pltpu.make_async_copy(meta_v, meta, meta_sem).start()

    def products(h, begin=0, end=SLOTS):
        def some(i):
            for j in range(GROUP):
                n = i * GROUP + j
                got = jnp.dot(stripe[h][meta[0, n]], tiles[n], preferred_element_type=jnp.float32)
                parts[h, n] = got + parts[h, meta[1, n]]
        loop(begin // GROUP, end // GROUP, some)

    def own(h, s, e):
        return parts[h, meta[2, 2 * s + e]]

    def skips(h, far):
        return h == 1 and far in JOINS

    def message(h, e, way, far):
        slot = (h, e, way, far - 1)
        return copy(
            sums_out.at[slot], sums_in.at[slot], s_send.at[slot], s_recv.at[slot], (col(SIGN[way] * (2 if skips(h, far) else 1)), r)
        )

    def arrives(h, before, far):
        return before - far == (2 if skips(h, before) else 1)

    def received(h, e, way, far):
        message(h, e, way, far).wait_recv()
        return sums_in[h, e, way, far - 1].astype(jnp.float32)

    def chain(h, far):
        for e in range(2):
            for way in range(2):
                most = farthest(e, way)
                if far <= most:
                    value = own(h, col(SIGN[way] * far), e)
                    for before in (far + 1, far + 2):
                        if before <= most and arrives(h, before, far):
                            value = value + received(h, e, way, before)
                    sums_out[h, e, way, far - 1] = value.astype(jnp.bfloat16)
                    message(h, e, way, far).start()

    def finish(h):
        for e in range(2):
            value = own(h, c, e)
            for way in range(2):
                for before in (1, 2):
                    if arrives(h, before, 0):
                        value = value + received(h, e, way, before)
            node_t[h * BLK:(h + 1) * BLK, e * BLK:(e + 1) * BLK] = value

    def sums_sent(h):
        for e in range(2):
            for way in range(2):
                for far in range(1, farthest(e, way) + 1):
                    message(h, e, way, far).wait_send()

    def joined(part):
        return jnp.concatenate([
            jnp.concatenate([part(h, e).astype(jnp.bfloat16) for e in range(2)], axis=1) for h in range(2)
        ], axis=0)

    def weight_near():
        def at(s):
            terms = joined(lambda h, e: own(h, s, e))
            return jnp.dot(terms, feats[s], preferred_element_type=jnp.float32)

        total[...] = at(c)

        def both(j):
            total[...] += at(col(j)) + at(col(-j))

        loop(1, RADIUS, both)

    def weight_far():
        got = total[...]
        for way in range(2):
            terms = joined(lambda h, e: sums_out[h, e, way, RADIUS - 1])
            got = got + jnp.dot(terms, feats[col(SIGN[way] * RADIUS)], preferred_element_type=jnp.float32)
        got = got.reshape(N_ROW, F // N_ROW, F)
        dw[...] = jnp.concatenate([got[:, :, :BLK], got[:, :, BLK:]], axis=1).astype(jnp.bfloat16)

    def term(at):
        return copy(dw.at[at], plane_in.at[r], a_send.at[at], a_recv.at[r], (c, at))

    def term_from(at):
        return copy(dw.at[at], plane_in.at[at], a_send.at[at], a_recv.at[at], (c, at))

    def along(at):
        return copy(line.at[c], line.at[c], z_send.at[at], z_recv.at[c], (at, r))

    def along_from(at):
        return copy(line.at[at], line.at[at], z_send.at[at], z_recv.at[at], (at, r))

    def back(at):
        return copy(done.at[r], done.at[r], b_send.at[at], b_recv.at[r], (c, at))

    def back_from(at):
        return copy(done.at[at], done.at[at], b_send.at[at], b_recv.at[at], (c, at))

    def share_plane():
        loop(1, N_ROW, lambda d: term(row(d)).start())
        plane_in[r] = dw[r]

    def share_line():
        loop(1, N_ROW, lambda d: term_from(row(d)).wait_recv())
        line[c] = jnp.sum(plane_in[...].astype(jnp.float32), axis=0).astype(jnp.bfloat16)
        loop(1, N_COL, lambda d: along(col(d)).start())

    def share_back():
        loop(1, N_COL, lambda d: along_from(col(d)).wait_recv())
        done[r] = jnp.sum(line[...].astype(jnp.float32), axis=0).astype(jnp.bfloat16)
        loop(1, N_ROW, lambda d: back(row(d)).start())

    gather_start(0)
    feature_step(0)
    positions()
    feature_step(1)
    gather_first(0)
    gather_start(1)
    feature_step(2)
    gather_second(0, 0)
    feature_step(3)
    gather_first(1)
    gather_second(0, 1)
    gather_second(0, 2)
    feature_step(4)
    fetches[4].wait()
    fetches[5].wait()
    pltpu.make_async_copy(meta_v, meta, meta_sem).wait()
    gather_end(0)
    products(0, 0, SLOTS // 2)
    feature_step(5)
    gather_second(1, 0)
    gather_second(1, 1)
    products(0, SLOTS // 2, SLOTS)
    chain(0, 8)
    feature_step(6)
    gather_second(1, 2)
    gather_end(1)
    products(1, 0, SLOTS // 2)
    chain(0, 7)
    products(1, SLOTS // 2, SLOTS)
    chain(1, 8)
    feature_end()
    weight_near()
    chain(0, 6)
    chain(1, 7)
    weight_far()
    share_plane()
    chain(0, 5)
    chain(1, 6)
    gather_sent(0)
    chain(0, 4)
    chain(1, 5)
    share_line()
    gather_sent(1)
    chain(0, 3)
    chain(1, 4)
    feature_sent()
    chain(0, 2)
    chain(1, 3)
    chain(1, 1)
    chain(0, 1)
    share_back()
    chain(1, 2)
    finish(0)
    sums_sent(0)
    finish(1)
    node = jnp.transpose(node_t[...])
    high = node.astype(jnp.bfloat16)
    low = (node - high.astype(jnp.float32)).astype(jnp.bfloat16)
    input_out[...] = sum(
        lax.dot_general(half, weight_ref[...], (((1,), (1,)), ((), ())), preferred_element_type=jnp.float32)
        for half in (high, low)
    ).astype(jnp.bfloat16)
    sums_sent(1)
    loop(1, N_ROW, lambda d: term(row(d)).wait_send())
    loop(1, N_COL, lambda d: along(col(d)).wait_send())
    loop(1, N_ROW, lambda d: back_from(row(d)).wait_recv())
    whole = done[...].astype(jnp.float32)
    weight_out[...] = jnp.concatenate(
        [whole[:, :F // N_ROW], whole[:, F // N_ROW:]], axis=2
    ).reshape(F, F)
    loop(1, N_ROW, lambda d: back(row(d)).wait_send())


def place(input_ref, weight_ref, input_out, weight_out):
    input_out[...] = input_ref[...]
    weight_out[...] = jnp.transpose(weight_ref[...])


def on_device(out_grad, relu_mask, features, weight, tile_values, tile_index, tile_count):
    vmem = pl.BlockSpec(memory_space=pltpu.VMEM)
    anywhere = pl.BlockSpec(memory_space=pl.ANY)
    dma = pltpu.SemaphoreType.DMA
    bf16, f32, i32 = jnp.bfloat16, jnp.float32, jnp.int32
    input_grad, weight_t = pl.pallas_call(
        kernel,
        name="layer_backward",
        out_shape=(jax.ShapeDtypeStruct((F, F), bf16), jax.ShapeDtypeStruct((F, F), f32)),
        in_specs=[pl.BlockSpec(memory_space=pltpu.SMEM)] + [anywhere] * 6,
        out_specs=(vmem, vmem),
        scratch_shapes=[
            pltpu.VMEM((1, SLOTS), i32),
            pltpu.VMEM((8, BLK), i32),
            pltpu.SMEM((8, BLK), i32),
            pltpu.VMEM((F, F), bf16),
            pltpu.VMEM((F, F), i32),
            pltpu.VMEM((N_COL, F, F), bf16),
            pltpu.VMEM((F, F), bf16),
            pltpu.VMEM((SLOTS, BLK, BLK), bf16),
            pltpu.VMEM((STRIPE, BLK, BLK), bf16),
            pltpu.VMEM((STRIPE, BLK, BLK), bf16),
            pltpu.VMEM((2, SLOTS + 1, BLK, BLK), f32),
            pltpu.VMEM((2, 2, 2, HALF, BLK, BLK), bf16),
            pltpu.VMEM((2, 2, 2, HALF, BLK, BLK), bf16),
            pltpu.VMEM((F, F), f32),
            pltpu.VMEM((F, F), f32),
            pltpu.VMEM((N_ROW, 2 * F // N_ROW, BLK), bf16),
            pltpu.VMEM((N_ROW, 2 * F // N_ROW, BLK), bf16),
            pltpu.VMEM((N_COL, 2 * F // N_ROW, BLK), bf16),
            pltpu.VMEM((N_ROW, 2 * F // N_ROW, BLK), bf16),
            dma((6,)), dma, dma((2, 31)), dma((2, N_ROW)), dma((PIECES, 2, RADIUS)), dma((PIECES, N_COL)),
            dma((2, 2, 2, HALF)), dma((2, 2, 2, HALF)),
            dma((N_ROW,)), dma((N_ROW,)), dma((N_COL,)), dma((N_COL,)), dma((N_ROW,)), dma((N_ROW,)),
        ],
        compiler_params=pltpu.CompilerParams(
            collective_id=0, has_side_effects=True, vmem_limit_bytes=60 * 2**20
        ),
        cost_estimate=pl.CostEstimate(flops=2 * 10**9, bytes_accessed=8 * 2**20, transcendentals=0),
    )(
        tile_count, tile_index.reshape(1, SLOTS), out_grad, relu_mask, features, weight,
        tile_values.reshape(SLOTS, BLK, BLK),
    )
    return pl.pallas_call(
        place,
        name="place",
        out_shape=(jax.ShapeDtypeStruct((F, F), bf16), jax.ShapeDtypeStruct((F, F), f32)),
        in_specs=[vmem, vmem],
        out_specs=(vmem, vmem),
    )(input_grad, weight_t)


def solution(mesh):
    placed = (
        P(("col", "row"), None),
        P(("col", "row"), None),
        P(("col", "row"), None),
        P(),
        P("col", "row", None, None, None),
        P("col", "row", None),
        P("col", "row"),
    )
    return jax.shard_map(
        on_device,
        mesh=mesh,
        in_specs=placed,
        out_specs=(P(("col", "row"), None), P()),
        check_vma=False,
    )
```

```python
import jax
import jax.numpy as jnp
from jax import lax
from jax.experimental import pallas as pl
from jax.experimental.pallas import tpu as pltpu
from jax.sharding import PartitionSpec as P

MESH = pl.DeviceIdType.MESH
BLK = 128
F = 256
SLOTS = 96
N_COL = 16
N_ROW = 32
COLB = 32
STRIPE = 64
HALF = N_COL // 2
GROUP = 16
PIECES = 2
PIECE = F // PIECES
RADIUS = 7
JOINS = (2,)
SIGN = (1, -1)


def farthest(e, way):
    return HALF if way == e % 2 else HALF - 1


def loop(begin, end, f):
    def one(i, _):
        f(i)
        return 0
    lax.fori_loop(begin, end, one, 0)


def kernel(
    count, index_hbm, grad_hbm, mask_hbm, feat_hbm, weight_hbm, tiles_hbm,
    input_out, weight_out,
    index_ref, meta_v, meta, grad_ref, mask_ref, feats, weight_ref, tiles, stripe_0, stripe_1, parts,
    sums_out, sums_in, node_t, total, dw, plane_in, line, done,
    load_sem, meta_sem, g_send, g_recv, f_send, f_recv, s_send, s_recv,
    a_send, a_recv, z_send, z_recv, b_send, b_recv,
):
    c = lax.axis_index("col")
    r = lax.axis_index("row")
    x, y, k = lax.div(r, 8), lax.rem(lax.div(r, 2), 4), lax.rem(r, 2)
    stripe = (stripe_0, stripe_1)

    def col(d):
        return lax.rem(c + d + N_COL, N_COL)

    def row(d):
        return lax.rem(r + d, N_ROW)

    def copy(src, dst, send, recv, device):
        return pltpu.make_async_remote_copy(
            src_ref=src, dst_ref=dst, send_sem=send, recv_sem=recv,
            device_id=device, device_id_type=MESH,
        )

    fetches = [
        pltpu.make_async_copy(source, target, load_sem.at[i])
        for i, (source, target) in enumerate((
            (grad_hbm, grad_ref), (mask_hbm, mask_ref), (index_hbm, index_ref),
            (feat_hbm, feats.at[c]), (weight_hbm, weight_ref), (tiles_hbm, tiles),
        ))
    ]
    for fetch in fetches:
        fetch.start()

    barrier = pltpu.get_barrier_semaphore()
    loop(1, N_COL, lambda d: pl.semaphore_signal(barrier, inc=1, device_id=(col(d), r), device_id_type=MESH))
    loop(1, N_ROW, lambda d: pl.semaphore_signal(barrier, inc=1, device_id=(c, row(d)), device_id_type=MESH))

    fetches[0].wait()
    fetches[1].wait()
    grad = grad_ref[...].astype(jnp.float32) * mask_ref[...].astype(jnp.float32)
    grad_t = jnp.transpose(grad).astype(jnp.bfloat16)
    for h in range(2):
        for e in range(2):
            stripe[h][2 * r + e] = grad_t[h * BLK:(h + 1) * BLK, e * BLK:(e + 1) * BLK]
        parts[h, SLOTS] = jnp.zeros((BLK, BLK), jnp.float32)
    fetches[2].wait()
    fetches[3].wait()

    pl.semaphore_wait(barrier, N_ROW - 1 + N_COL - 1)

    def peer(a, b):
        dx = a * (1 - k) + b * k
        dy = a * k + b * (1 - k)
        return (lax.rem(x + dx, 4) * 4 + lax.rem(y + dy, 4)) * 2 + k

    sibling = r + 1 - 2 * k

    def unit(h, at):
        return stripe[h].at[pl.ds(2 * at, 2)]

    def push(h, at, target, number):
        copy(unit(h, at), unit(h, at), g_send.at[h, number], g_recv.at[h, at], (c, target)).start()

    def arrived(h, at):
        copy(unit(h, at), unit(h, at), g_send.at[h, 0], g_recv.at[h, at], (c, sibling)).wait_recv()

    order = (1, 3, 2)

    def gather_start(h):
        for i, a in enumerate(order):
            push(h, r, peer(a, 0), i)
        for i, b in enumerate(order):
            push(h, r, peer(0, b), 3 + i)
        push(h, r, sibling, 6)

    def gather_first(h):
        for i, a in enumerate(order):
            at = peer(4 - a, 0)
            arrived(h, at)
            for j, b in enumerate(order):
                push(h, at, peer(0, b), 7 + 4 * i + j)
            push(h, at, sibling, 7 + 4 * i + 3)

    def gather_second(h, j):
        for i, a in enumerate((0,) + order):
            at = peer((4 - a) % 4, 4 - order[j])
            arrived(h, at)
            push(h, at, sibling, 19 + 4 * j + i)

    def gather_end(h):
        loop(0, N_ROW // 2, lambda i: arrived(h, 2 * i + 1 - k))

    def gather_sent(h):
        loop(0, 31, lambda i: copy(
            unit(h, r), unit(h, r), g_send.at[h, i], g_recv.at[h, r], (c, sibling)).wait_send())

    def feature(q, way, far):
        origin = col(-SIGN[way] * far)
        held = feats.at[origin, pl.ds(q * PIECE, PIECE)]
        return copy(held, held, f_send.at[q, way, far], f_recv.at[q, origin], (col(SIGN[way]), r))

    def feature_step(far):
        for q in range(PIECES):
            for way in range(2):
                if far > 0:
                    feature(q, way, far).wait_recv()
                feature(q, way, far).start()

    def feature_end():
        for q in range(PIECES):
            for way in range(2):
                feature(q, way, RADIUS).wait_recv()

    def feature_sent():
        for q in range(PIECES):
            for way in range(2):
                loop(0, RADIUS, lambda far: feature(q, way, far).wait_send())

    def positions():
        index = index_ref[...]
        down = lax.broadcasted_iota(jnp.int32, (SLOTS, SLOTS), 0)
        across = lax.broadcasted_iota(jnp.int32, (SLOTS, SLOTS), 1)
        column = jnp.broadcast_to(lax.rem(index, COLB), (SLOTS, SLOTS))
        column_down = jnp.sum(jnp.where(down == across, column, 0), axis=1, keepdims=True)
        column_down = jnp.broadcast_to(column_down, (SLOTS, SLOTS))
        previous = jnp.max(
            jnp.where((column == column_down) & (down < across), down, -1), axis=0, keepdims=True
        )
        last = jnp.max(
            jnp.where((column_down == across) & (down < count[0, 0]), down, -1), axis=0, keepdims=True
        )
        meta_v[...] = jnp.zeros_like(meta_v)
        meta_v[0:1, 0:SLOTS] = lax.div(index, COLB)
        meta_v[1:2, 0:SLOTS] = jnp.where(previous < 0, SLOTS, previous)
        meta_v[2:3, 0:SLOTS] = jnp.where(last < 0, SLOTS, last)
        pltpu.make_async_copy(meta_v, meta, meta_sem).start()

    def products(h, begin=0, end=SLOTS):
        def some(i):
            for j in range(GROUP):
                n = i * GROUP + j
                got = jnp.dot(stripe[h][meta[0, n]], tiles[n], preferred_element_type=jnp.float32)
                parts[h, n] = got + parts[h, meta[1, n]]
        loop(begin // GROUP, end // GROUP, some)

    def own(h, s, e):
        return parts[h, meta[2, 2 * s + e]]

    def skips(h, far):
        return h == 1 and far in JOINS

    def message(h, e, way, far):
        slot = (h, e, way, far - 1)
        return copy(
            sums_out.at[slot], sums_in.at[slot], s_send.at[slot], s_recv.at[slot], (col(SIGN[way] * (2 if skips(h, far) else 1)), r)
        )

    def arrives(h, before, far):
        return before - far == (2 if skips(h, before) else 1)

    def received(h, e, way, far):
        message(h, e, way, far).wait_recv()
        return sums_in[h, e, way, far - 1].astype(jnp.float32)

    def chain(h, far):
        for e in range(2):
            for way in range(2):
                most = farthest(e, way)
                if far <= most:
                    value = own(h, col(SIGN[way] * far), e)
                    for before in (far + 1, far + 2):
                        if before <= most and arrives(h, before, far):
                            value = value + received(h, e, way, before)
                    sums_out[h, e, way, far - 1] = value.astype(jnp.bfloat16)
                    message(h, e, way, far).start()

    def finish(h):
        for e in range(2):
            value = own(h, c, e)
            for way in range(2):
                for before in (1, 2):
                    if arrives(h, before, 0):
                        value = value + received(h, e, way, before)
            node_t[h * BLK:(h + 1) * BLK, e * BLK:(e + 1) * BLK] = value

    def sums_sent(h):
        for e in range(2):
            for way in range(2):
                for far in range(1, farthest(e, way) + 1):
                    message(h, e, way, far).wait_send()

    def joined(part):
        return jnp.concatenate([
            jnp.concatenate([part(h, e).astype(jnp.bfloat16) for e in range(2)], axis=1) for h in range(2)
        ], axis=0)

    def weight_near():
        def at(s):
            terms = joined(lambda h, e: own(h, s, e))
            return jnp.dot(terms, feats[s], preferred_element_type=jnp.float32)

        total[...] = at(c)

        def both(j):
            total[...] += at(col(j)) + at(col(-j))

        loop(1, RADIUS, both)

    def weight_far():
        got = total[...]
        for way in range(2):
            terms = joined(lambda h, e: sums_out[h, e, way, RADIUS - 1])
            got = got + jnp.dot(terms, feats[col(SIGN[way] * RADIUS)], preferred_element_type=jnp.float32)
        got = got.reshape(N_ROW, F // N_ROW, F)
        dw[...] = jnp.concatenate([got[:, :, :BLK], got[:, :, BLK:]], axis=1).astype(jnp.bfloat16)

    def term(at):
        return copy(dw.at[at], plane_in.at[r], a_send.at[at], a_recv.at[r], (c, at))

    def term_from(at):
        return copy(dw.at[at], plane_in.at[at], a_send.at[at], a_recv.at[at], (c, at))

    def along(at):
        return copy(line.at[c], line.at[c], z_send.at[at], z_recv.at[c], (at, r))

    def along_from(at):
        return copy(line.at[at], line.at[at], z_send.at[at], z_recv.at[at], (at, r))

    def back(at):
        return copy(done.at[r], done.at[r], b_send.at[at], b_recv.at[r], (c, at))

    def back_from(at):
        return copy(done.at[at], done.at[at], b_send.at[at], b_recv.at[at], (c, at))

    def share_plane():
        loop(1, N_ROW, lambda d: term(row(d)).start())
        plane_in[r] = dw[r]

    def share_line():
        loop(1, N_ROW, lambda d: term_from(row(d)).wait_recv())
        line[c] = jnp.sum(plane_in[...].astype(jnp.float32), axis=0).astype(jnp.bfloat16)
        loop(1, N_COL, lambda d: along(col(d)).start())

    def share_back():
        loop(1, N_COL, lambda d: along_from(col(d)).wait_recv())
        done[r] = jnp.sum(line[...].astype(jnp.float32), axis=0).astype(jnp.bfloat16)
        loop(1, N_ROW, lambda d: back(row(d)).start())

    gather_start(0)
    feature_step(0)
    positions()
    feature_step(1)
    gather_first(0)
    gather_start(1)
    feature_step(2)
    gather_second(0, 0)
    feature_step(3)
    gather_first(1)
    gather_second(0, 1)
    gather_second(0, 2)
    feature_step(4)
    fetches[4].wait()
    fetches[5].wait()
    pltpu.make_async_copy(meta_v, meta, meta_sem).wait()
    gather_end(0)
    products(0, 0, SLOTS // 2)
    feature_step(5)
    gather_second(1, 0)
    gather_second(1, 1)
    products(0, SLOTS // 2, SLOTS)
    chain(0, 8)
    feature_step(6)
    gather_second(1, 2)
    gather_end(1)
    products(1, 0, SLOTS // 2)
    chain(0, 7)
    products(1, SLOTS // 2, SLOTS)
    chain(1, 8)
    feature_end()
    weight_near()
    chain(0, 6)
    chain(1, 7)
    weight_far()
    share_plane()
    chain(0, 5)
    chain(1, 6)
    gather_sent(0)
    chain(0, 4)
    chain(1, 5)
    share_line()
    gather_sent(1)
    chain(0, 3)
    chain(1, 4)
    feature_sent()
    chain(0, 2)
    chain(1, 3)
    chain(1, 1)
    chain(0, 1)
    share_back()
    chain(1, 2)
    finish(0)
    sums_sent(0)
    finish(1)
    node = jnp.transpose(node_t[...])
    high = node.astype(jnp.bfloat16)
    low = (node - high.astype(jnp.float32)).astype(jnp.bfloat16)
    input_out[...] = sum(
        lax.dot_general(half, weight_ref[...], (((1,), (1,)), ((), ())), preferred_element_type=jnp.float32)
        for half in (high, low)
    ).astype(jnp.bfloat16)
    sums_sent(1)
    loop(1, N_ROW, lambda d: term(row(d)).wait_send())
    loop(1, N_COL, lambda d: along(col(d)).wait_send())
    loop(1, N_ROW, lambda d: back_from(row(d)).wait_recv())
    whole = done[...].astype(jnp.float32)
    weight_out[...] = jnp.concatenate(
        [whole[:, :F // N_ROW], whole[:, F // N_ROW:]], axis=2
    ).reshape(F, F)
    loop(1, N_ROW, lambda d: back(row(d)).wait_send())


def place(input_ref, weight_ref, input_out, weight_out):
    input_out[...] = input_ref[...]
    weight_out[...] = jnp.transpose(weight_ref[...])


def on_device(out_grad, relu_mask, features, weight, tile_values, tile_index, tile_count):
    vmem = pl.BlockSpec(memory_space=pltpu.VMEM)
    anywhere = pl.BlockSpec(memory_space=pl.ANY)
    dma = pltpu.SemaphoreType.DMA
    bf16, f32, i32 = jnp.bfloat16, jnp.float32, jnp.int32
    input_grad, weight_t = pl.pallas_call(
        kernel,
        name="layer_backward",
        out_shape=(jax.ShapeDtypeStruct((F, F), bf16), jax.ShapeDtypeStruct((F, F), f32)),
        in_specs=[pl.BlockSpec(memory_space=pltpu.SMEM)] + [anywhere] * 6,
        out_specs=(vmem, vmem),
        scratch_shapes=[
            pltpu.VMEM((1, SLOTS), i32),
            pltpu.VMEM((8, BLK), i32),
            pltpu.SMEM((8, BLK), i32),
            pltpu.VMEM((F, F), bf16),
            pltpu.VMEM((F, F), i32),
            pltpu.VMEM((N_COL, F, F), bf16),
            pltpu.VMEM((F, F), bf16),
            pltpu.VMEM((SLOTS, BLK, BLK), bf16),
            pltpu.VMEM((STRIPE, BLK, BLK), bf16),
            pltpu.VMEM((STRIPE, BLK, BLK), bf16),
            pltpu.VMEM((2, SLOTS + 1, BLK, BLK), f32),
            pltpu.VMEM((2, 2, 2, HALF, BLK, BLK), bf16),
            pltpu.VMEM((2, 2, 2, HALF, BLK, BLK), bf16),
            pltpu.VMEM((F, F), f32),
            pltpu.VMEM((F, F), f32),
            pltpu.VMEM((N_ROW, 2 * F // N_ROW, BLK), bf16),
            pltpu.VMEM((N_ROW, 2 * F // N_ROW, BLK), bf16),
            pltpu.VMEM((N_COL, 2 * F // N_ROW, BLK), bf16),
            pltpu.VMEM((N_ROW, 2 * F // N_ROW, BLK), bf16),
            dma((6,)), dma, dma((2, 31)), dma((2, N_ROW)), dma((PIECES, 2, RADIUS)), dma((PIECES, N_COL)),
            dma((2, 2, 2, HALF)), dma((2, 2, 2, HALF)),
            dma((N_ROW,)), dma((N_ROW,)), dma((N_COL,)), dma((N_COL,)), dma((N_ROW,)), dma((N_ROW,)),
        ],
        compiler_params=pltpu.CompilerParams(
            collective_id=0, has_side_effects=True, vmem_limit_bytes=60 * 2**20
        ),
        cost_estimate=pl.CostEstimate(flops=2 * 10**9, bytes_accessed=8 * 2**20, transcendentals=0),
    )(
        tile_count, tile_index.reshape(1, SLOTS), out_grad, relu_mask, features, weight,
        tile_values.reshape(SLOTS, BLK, BLK),
    )
    return pl.pallas_call(
        place,
        name="place",
        out_shape=(jax.ShapeDtypeStruct((F, F), bf16), jax.ShapeDtypeStruct((F, F), f32)),
        in_specs=[vmem, vmem],
        out_specs=(vmem, vmem),
    )(input_grad, weight_t)


def solution(mesh):
    placed = (
        P(("col", "row"), None),
        P(("col", "row"), None),
        P(("col", "row"), None),
        P(),
        P("col", "row", None, None, None),
        P("col", "row", None),
        P("col", "row"),
    )
    return jax.shard_map(
        on_device,
        mesh=mesh,
        in_specs=placed,
        out_specs=(P(("col", "row"), None), P()),
        check_vma=False,
    )
```
